256 devices in a mesh: elem: 32 (over z, x_hi, core), mode: 8 (over y, x_lo).
Axes of the slice: x: 4 (x_hi: 2, x_lo: 2; x = x_hi * 2 + x_lo), y: 4, z: 8, core: 2. Of those that a mesh axis runs over, the one named last changes fastest.
Arguments:
- velocity: float32 [1024, 1024, 128], P(None, ('elem', 'mode')), may hold values from -6 to 6
- previous: float32 [1024, 1024, 128], P('mode', 'elem'), may hold values from -6 to 6
- derivative: float32 [128, 128], replicated, may hold values from -0.5 to 0.5
- stiffness: float32 [128, 128], replicated, as said below
- coupling: float32 [4, 128, 128], replicated, may hold values from -0.25 to 0.25
- reaction: float32 [1024], P('elem'), may hold values from 0.5 to 4
- axial_weight: float32 [1024], P('elem'), may hold values from 0.5 to 4
- neighbours: int32 [1024, 4], P('elem'), may hold values from -1 to 1023, as said below
Outputs:
- solution: float32 [1024, 1024, 128], P('mode', 'elem')
The draws below stay inside these ranges and needn't reach their ends.
Inputs may be any that keep to these rules, and one draw needn't show every extreme that they name: `stiffness`: symmetric with a positive diagonal. `neighbours`: elements lie on a grid of 8 rows, periodic along the rows, and 4 columns a group of 32 elements, groups in order along the columns with walls at both ends. A group's first 8 elements form its first column and its last 8 its last column; a neighbour in another group is in the next or previous group, among its first or last 8 elements.
All inputs are finite; a program needn't handle non-finite values.
Results may differ from the reference program's by a relative error of at most 0.0001.
Values sent between devices are 32-bit elements; how exact they have to be, the bound alone decides.
No kernel may reach another device: no remote copies, remote signals or barrier semaphores. Data moves between devices by JAX's collectives and lax.ppermute only.
A program may use at most 128 MiB of HBM per device.

```python
import math
import jax
import jax.numpy as jnp
from jax import lax

Q = 128
NZ = 1024
EG = 32
EY = 8
E = 1024


def draw_stiffness(key, part):
    first_key, second_key = jax.random.split(jax.random.fold_in(key, 11))
    diagonal = jax.random.uniform(first_key, (Q,), jnp.float32, 2.0, 6.0)
    noise = jax.random.normal(second_key, (Q, Q), jnp.float32) * (0.3 / math.sqrt(Q))
    return jnp.diag(diagonal) + 0.5 * (noise + noise.T)


def draw_neighbours(key, part):
    groups = E // EG
    columns = EG // EY
    places = jnp.arange(EG, dtype=jnp.int32)
    column_of = places // EY
    column_kind = jnp.where(column_of == 0, 0, jnp.where(column_of == columns - 1, 2, 1)).astype(jnp.int32)

    def arrange(group_index):
        shuffle = jax.random.permutation(jax.random.fold_in(jax.random.fold_in(key, 23), group_index), EG).astype(jnp.int32)
        slot_place = jnp.argsort(column_kind * EG + shuffle, stable=True).astype(jnp.int32)
        place_slot = jnp.argsort(slot_place, stable=True).astype(jnp.int32)
        return (slot_place, place_slot)
    orders, slots = jax.vmap(arrange)(jnp.arange(groups, dtype=jnp.int32))
    element_place = orders.reshape(-1)
    group_of = jnp.arange(E, dtype=jnp.int32) // EG
    grid_col = group_of * columns + element_place // EY
    grid_row = element_place % EY
    total_cols = groups * columns

    def element_at(column_at, row_at):
        group_at = column_at // columns
        place_at = column_at % columns * EY + row_at
        return group_at * EG + slots[group_at, place_at]
    left_id = jnp.where(grid_col > 0, element_at(jnp.maximum(grid_col - 1, 0), grid_row), -1)
    right_id = jnp.where(grid_col < total_cols - 1, element_at(jnp.minimum(grid_col + 1, total_cols - 1), grid_row), -1)
    down_id = element_at(grid_col, (grid_row + EY - 1) % EY)
    up_id = element_at(grid_col, (grid_row + 1) % EY)
    return jnp.stack([left_id, right_id, down_id, up_id], axis=1).astype(jnp.int32)


def block_scale(key, dims, cuts, smallest, top_value):
    gain, own = 1.0, jax.random.fold_in(key, 6)
    for dim, parts in cuts:
        heights = jnp.exp(jax.random.uniform(jax.random.fold_in(own, dim), (parts,), jnp.float32, smallest / len(cuts), top_value / len(cuts)))
        gain = gain * jnp.repeat(heights, dims[dim] // parts).reshape([-1 if axis == dim else 1 for axis in range(len(dims))])
    return gain


def normal_values(rng, extent, width, most, cuts=(), kind=jnp.bfloat16):
    array = jax.random.normal(rng, extent, jnp.float32) * width
    if len(cuts) > 0:
        array = block_scale(rng, extent, cuts, -0.22, 0.18) * array
    return jnp.clip(array, min=-most, max=most).astype(kind)


def setup_inputs(seed: int = 0) -> dict:
    key_of = jax.random.split(jax.random.key(seed), 9)
    velocity = normal_values(key_of[0], (NZ, E, Q), 1.0, 6.0, ((1, 256),), jnp.float32)
    previous = normal_values(key_of[1], (NZ, E, Q), 1.0, 6.0, ((0, 8), (1, 32)), jnp.float32)
    derivative = normal_values(key_of[2], (Q, Q), Q ** -0.5, 0.5, (), jnp.float32)
    stiffness = draw_stiffness(jax.random.fold_in(key_of[8], 71), 0)
    coupling = normal_values(key_of[4], (4, Q, Q), (4 * Q) ** -0.5, 0.25, (), jnp.float32)
    reaction = jnp.clip(jnp.exp(math.log(4.0) - 2.0794415 * jax.random.uniform(key_of[5], (E,), jnp.float32) ** block_scale(key_of[5], (E,), ((0, 32),), -0.2, 0.2)), 0.5, 4.0)
    axial_weight = jnp.clip(jnp.exp(math.log(4.0) - 2.0794415 * jax.random.uniform(key_of[6], (E,), jnp.float32) ** block_scale(key_of[6], (E,), ((0, 32),), -0.2, 0.2)), 0.5, 4.0)
    neighbours = draw_neighbours(jax.random.fold_in(key_of[8], 71), 0)
    return dict(velocity=velocity, previous=previous, derivative=derivative, stiffness=stiffness, coupling=coupling, reaction=reaction, axial_weight=axial_weight, neighbours=neighbours)


highest = lax.Precision.HIGHEST
dt_step = 0.5
first_weight = 0.7
second_weight = 1.1


def row_shift(count):
    rows = jnp.arange(count, dtype=jnp.int32)
    half = count // 2
    waves = jnp.where(rows <= half, rows, rows - half).astype(jnp.float32)
    return 4.0 * (waves / half) ** 2


def reference(velocity, previous, derivative, stiffness, coupling, reaction, axial_weight, neighbours):
    slope = jnp.einsum('zeq,pq->zep', velocity, derivative, precision=highest)
    product = velocity - dt_step * velocity * slope
    spectrum = jnp.fft.rfft(product, axis=0)
    half = NZ // 2
    rhs = jnp.concatenate([spectrum.real[:half], spectrum.real[half:half + 1], spectrum.imag[1:half]], axis=0) * (NZ ** -0.5)
    shifts = row_shift(NZ).astype(rhs.dtype)
    present = neighbours >= 0
    near_index = jnp.where(present, neighbours, 0).astype(jnp.int32)
    face_mask = present.astype(rhs.dtype)
    stiff_diag = jnp.diagonal(stiffness)

    def apply(field, shift_rows):
        result = jnp.einsum('req,pq->rep', field, stiffness, precision=highest)
        result = result + (reaction[None, :, None] + shift_rows[:, None, None] * axial_weight[None, :, None]) * field
        for side_index in range(4):
            beside = jnp.take(field, near_index[:, side_index], axis=1) * face_mask[None, :, side_index, None]
            result = result + jnp.einsum('req,pq->rep', beside, coupling[side_index], precision=highest)
        return result

    def sweep_block(inputs):
        rhs_rows, start_rows, shift_rows = inputs
        inverse = 1.0 / (stiff_diag[None, None, :] + reaction[None, :, None] + shift_rows[:, None, None] * axial_weight[None, :, None])
        first = start_rows + first_weight * inverse * (rhs_rows - apply(start_rows, shift_rows))
        return first + second_weight * inverse * (rhs_rows - apply(first, shift_rows))

    blocks = 16
    rows_block = NZ // blocks
    result = lax.map(sweep_block, (rhs.reshape(blocks, rows_block, E, Q), previous.reshape(blocks, rows_block, E, Q), shifts.reshape(blocks, rows_block)))
    return result.reshape(NZ, E, Q)
```

```python
import functools
import math

import jax
import jax.numpy as jnp
import numpy as np
from jax import lax
from jax.experimental import pallas as pl
from jax.experimental.pallas import tpu as pltpu
from jax.sharding import PartitionSpec as P

dt_step = 0.5
first_weight = 0.7
second_weight = 1.1

chunks = 1


def split(x):
    high = x.astype(jnp.bfloat16)
    low = (x - high.astype(jnp.float32)).astype(jnp.bfloat16)
    return high, low


def pair(x):
    return jnp.concatenate(split(x), axis=1)


def pair_weight(w):
    high, low = split(w)
    return jnp.concatenate(
        [jnp.concatenate([high, high], axis=1), jnp.concatenate([low, low], axis=1)], axis=0
    )


def dot_nt(x, w):
    return lax.dot_general(x, w, (((1,), (1,)), ((), ())), preferred_element_type=jnp.float32)


def times(x, w):
    y = dot_nt(x, w)
    n = y.shape[1] // 2
    return y[:, :n] + y[:, n:]


@functools.cache
def dft_tables(planes):
    half, quarter = planes // 2, planes // 4
    rows = np.arange(planes)
    waves = np.where(rows <= half, rows, rows - half)

    def table(picked, count):
        z = np.arange(count)
        phase = (waves[picked][:, None] * z[None, :]) % planes
        angle = 2.0 * np.pi / planes * phase
        t = np.where((picked <= half)[:, None], np.cos(angle), -np.sin(angle)) * planes**-0.5
        high = t.astype(np.float32).astype(jnp.bfloat16)
        low = (t - high.astype(np.float64)).astype(np.float32).astype(jnp.bfloat16)
        return np.concatenate([high, low], axis=1)

    odd = table(rows[1::2], half)
    even = np.concatenate([table(rows[2::4], quarter), table(rows[0::4], quarter)], axis=0)
    return odd, even


def dft3(t, h, l):
    k = t.shape[1] // 2
    dot = functools.partial(jnp.dot, preferred_element_type=jnp.float32)
    return dot(t[:, :k], h) + dot(t[:, :k], l) + dot(t[:, k:], h)


def pack_kernel(prev, tail, head, sems):
    rim = head.shape[1]
    elems = prev.shape[1]
    copies = [
        pltpu.make_async_copy(prev.at[:, pl.ds(elems - rim, rim), :], tail, sems.at[0]),
        pltpu.make_async_copy(prev.at[:, pl.ds(0, rim), :], head, sems.at[1]),
    ]
    for c in copies:
        c.start()
    for c in copies:
        c.wait()


def spectrum_kernel(tile, tail, head, vel_hbm, der, odd_hbm, even_hbm, *refs):
    outs, (vel, odd_table, even_table, dh, dl, eh, el, stage, sems, table_sems, out_sems) = refs[:chunks], refs[chunks:]
    nodes = der.shape[0]
    local = dh.shape[1] // nodes
    planes = vel.shape[0] // local
    quarter = planes // 4
    tiles = quarter // tile
    devices = outs[0].shape[0]
    reads = []
    for t in range(tiles):
        here = []
        for j in range(4):
            rows = pl.ds((j * quarter + t * tile) * local, tile * local)
            here.append(pltpu.make_async_copy(vel_hbm.at[rows, :], vel.at[rows, :], sems.at[t, j]))
            here[-1].start()
        reads.append(here)
    table_reads = [
        pltpu.make_async_copy(odd_hbm, odd_table, table_sems.at[0]),
        pltpu.make_async_copy(even_hbm, even_table, table_sems.at[1]),
    ]
    for c in table_reads:
        c.start()
    weight = pair_weight(der[...])

    for t in range(tiles):
        for c in reads[t]:
            c.wait()
        for e in range(local):
            cols = slice(e * nodes, (e + 1) * nodes)
            v = jnp.concatenate(
                [
                    vel[pl.ds((j * quarter + t * tile) * local + e, tile, stride=local), :]
                    for j in range(4)
                ],
                axis=0,
            )
            p = v - dt_step * v * times(pair(v), weight)
            p0, p1, p2, p3 = (p[j * tile : (j + 1) * tile] for j in range(4))
            s0, s1 = p0 + p2, p1 + p3
            here, there = slice(t * tile, (t + 1) * tile), slice(quarter + t * tile, quarter + (t + 1) * tile)
            dh[here, cols], dl[here, cols] = split(p0 - p2)
            dh[there, cols], dl[there, cols] = split(p1 - p3)
            eh[here, cols], el[here, cols] = split(s0 - s1)
            eh[there, cols], el[there, cols] = split(s0 + s1)

    for c in table_reads:
        c.wait()
    rows = stage.shape[3]
    group = 2
    writes = []
    for g in range(0, local, group):
        cols = slice(g * nodes, (g + group) * nodes)
        odd = dft3(odd_table[...], dh[:, cols], dl[:, cols])
        two = dft3(even_table[:quarter], eh[:quarter, cols], el[:quarter, cols])
        zero = dft3(even_table[quarter:], eh[quarter:, cols], el[quarter:, cols])
        for values, offset, stride in ((odd, 1, 2), (two, 2, 4), (zero, 0, 4)):
            n = rows // stride
            for m in range(devices):
                for c in range(chunks):
                    at = (m * chunks + c) * n
                    for e in range(group):
                        stage[c, m, g + e, pl.ds(offset, n, stride=stride), :] = values[
                            at : at + n, e * nodes : (e + 1) * nodes
                        ]
        for c in range(chunks):
            writes.append(
                pltpu.make_async_copy(
                    stage.at[c, :, pl.ds(g, group)], outs[c].at[:, pl.ds(g, group)], out_sems.at[c, g // group]
                )
            )
            writes[-1].start()
    for c in writes:
        c.wait()


def row_shift(first_row, count, planes, lanes):
    rows = first_row + lax.broadcasted_iota(jnp.int32, (count, lanes), 0)
    half = planes // 2
    waves = jnp.where(rows <= half, rows, rows - half).astype(jnp.float32)
    return 4.0 * (waves * (1.0 / half)) ** 2


def diagonal(stiff):
    n = stiff.shape[0]
    eye = lax.broadcasted_iota(jnp.int32, (n, n), 0) == lax.broadcasted_iota(jnp.int32, (n, n), 1)
    return jnp.sum(jnp.where(eye, stiff, 0.0), axis=0, keepdims=True)


def start_kernel(planes, chunk, meta, near, reaction, axial, prev, left, right, stiff, coupling, out, h, y, y0, y1):
    elems, rows, nodes = out.shape
    rim = left.shape[1] // 1
    group = meta[0] * elems
    prev = prev.reshape(rows * elems, nodes)
    left = left.reshape(rows * rim, nodes)
    right = right.reshape(rows * rim, nodes)

    for e in range(rim):
        h[e] = pair(left[pl.ds(e, rows, stride=rim), :])
        h[rim + elems + e] = pair(right[pl.ds(e, rows, stride=rim), :])
    for e in range(elems):
        v = prev[pl.ds(e, rows, stride=elems), :]
        out[e] = v
        h[rim + e] = pair(v)
    step = 8

    def fill(dst, w, a, b):
        for i in range(a, b, step):
            x = h[i : i + step].reshape(step * rows, 2 * nodes)
            dst[i - a : i - a + step] = times(x, w).reshape(step, rows, nodes)

    fill(y0, pair_weight(coupling[0]), 0, rim + elems)
    fill(y1, pair_weight(coupling[1]), rim, rim + elems + rim)
    y0[rim + elems] = jnp.zeros((rows, nodes), jnp.float32)
    y1[rim + elems] = jnp.zeros((rows, nodes), jnp.float32)
    for f in (2, 3):
        fill(y.at[f - 2], pair_weight(coupling[f]), rim, rim + elems)
        y[f - 2, elems] = jnp.zeros((rows, nodes), jnp.float32)
    fill(y.at[2], pair_weight(stiff[...]), rim, rim + elems)

    shift = row_shift(meta[1] * (chunks * rows) + chunk * rows, rows, planes, nodes)
    diag = diagonal(stiff[...])

    def place(e, f, low, high):
        n = near[e, f]
        return jnp.where(n >= 0, jnp.clip(n - group + low, 0, high - 1), high)

    def combine(e, carry):
        v = out[e]
        scaling = reaction[e] + shift * axial[e]
        total = y[2, e] + scaling * v
        total += y0[place(e, 0, rim, rim + elems)] + y1[place(e, 1, 0, rim + elems)]
        total += y[0, place(e, 2, 0, elems)] + y[1, place(e, 3, 0, elems)]
        out[e] = v - first_weight * total / (diag + scaling)
        return carry

    lax.fori_loop(0, elems, combine, 0)


def first_kernel(planes, chunk, meta, reaction, axial, base, rhs, stiff, out, head, tail):
    elems, rows, nodes = base.shape
    rim = head.shape[0]
    shift = row_shift(meta[1] * (chunks * rows) + chunk * rows, rows, planes, nodes)
    diag = diagonal(stiff[...])
    for e in range(elems):
        scaling = reaction[e] + shift * axial[e]
        v = base[e] + first_weight * rhs[e] / (diag + scaling)
        out[e] = v
        if e < rim:
            head[e] = v
        if e >= elems - rim:
            tail[e - (elems - rim)] = v


def second_kernel(planes, chunk, meta, near, reaction, axial, first, rhs, stiff, coupling, *refs):
    out, rest, h, y, stage, sem = refs[-6:]
    elems, rows, nodes = first.shape
    rim = rest.shape[0] // 2
    inner = elems - 2 * rim
    group = meta[0] * elems
    for e in range(elems):
        h[e] = pair(first[e])
    step = 8

    def fill(f, w):
        for i in range(0, elems, step):
            y[f, i : i + step] = times(h[i : i + step].reshape(step * rows, 2 * nodes), w).reshape(step, rows, nodes)

    for f in range(4):
        fill(f, pair_weight(coupling[f]))
        y[f, elems] = jnp.zeros((rows, nodes), jnp.float32)
    fill(4, pair_weight(stiff[...]))
    shift = row_shift(meta[1] * (chunks * rows) + chunk * rows, rows, planes, nodes)
    diag = diagonal(stiff[...])

    def place(e, f):
        at = near[e, f] - group
        return jnp.where((at >= 0) & (at < elems), at, elems)

    def combine(e):
        v = first[e]
        scaling = reaction[e] + shift * axial[e]
        total = y[4, e] + scaling * v
        for f in range(4):
            total += y[f, place(e, f)]
        return v + second_weight * (rhs[e] - total) / (diag + scaling)

    flat = stage.reshape(rows * inner, nodes)
    for e in range(rim, elems - rim):
        flat[pl.ds(e - rim, rows, stride=inner), :] = combine(e)
    copy = pltpu.make_async_copy(stage, out.at[pl.ds(chunk * rows, rows), pl.ds(rim, inner), :], sem)
    copy.start()
    for e in range(rim):
        rest[e] = combine(e)
        rest[rim + e] = combine(elems - rim + e)
    copy.wait()


def finish_kernel(planes, chunk, meta, near, reaction, axial, rest, left, right, stiff, coupling, kept, out, h, y, stage, sems):
    elems = near.shape[0]
    rim, rows, nodes = left.shape
    group = meta[0] * elems
    for e in range(rim):
        h[e] = pair(left[e])
        h[rim + e] = pair(right[e])
    shift = row_shift(meta[1] * (chunks * rows) + chunk * rows, rows, planes, nodes)
    diag = diagonal(stiff[...])
    copies = []
    for f in range(2):
        y[f, :rim] = times(
            h[f * rim : (f + 1) * rim].reshape(rim * rows, 2 * nodes), pair_weight(coupling[f])
        ).reshape(rim, rows, nodes)
        y[f, rim] = jnp.zeros((rows, nodes), jnp.float32)
        first_elem = f * (elems - rim)
        flat = stage.at[f].reshape(rows * rim, nodes)
        for i in range(rim):
            e = first_elem + i
            n = near[e, f]
            at = n - group + rim if f == 0 else n - group - elems
            at = jnp.where((n >= 0) & (at >= 0) & (at < rim), at, rim)
            scaling = reaction[e] + shift * axial[e]
            values = rest[f * rim + i] - second_weight * y[f, at] / (diag + scaling)
            flat[pl.ds(i, rows, stride=rim), :] = values
        copies.append(
            pltpu.make_async_copy(stage.at[f], out.at[pl.ds(chunk * rows, rows), pl.ds(first_elem, rim), :], sems.at[f])
        )
        copies[-1].start()
    for c in copies:
        c.wait()


vmem = pl.BlockSpec(memory_space=pltpu.VMEM)
smem = pl.BlockSpec(memory_space=pltpu.SMEM)
hbm = pl.BlockSpec(memory_space=pltpu.HBM)
anywhere = pl.BlockSpec(memory_space=pl.ANY)


def call(kernel, name, outs, out_specs, in_specs, scratch, args, mib, us, aliases=None):
    return pl.pallas_call(
        kernel,
        out_shape=outs,
        in_specs=in_specs,
        out_specs=out_specs,
        scratch_shapes=scratch,
        compiler_params=pltpu.CompilerParams(vmem_limit_bytes=mib * 2**20),
        cost_estimate=pl.CostEstimate(flops=int(us * 1e9), bytes_accessed=int(us * 3e6), transcendentals=0),
        input_output_aliases=aliases or {},
        name=name,
    )(*args)


def body(velocity, previous, derivative, stiffness, coupling, reaction, axial_weight, neighbours):
    planes, local, nodes = velocity.shape
    own_rows, elems, _ = previous.shape
    rim = elems // 4
    rows = own_rows // chunks
    devices = planes // own_rows
    groups = lax.axis_size("elem")
    f32, bf16 = jnp.float32, jnp.bfloat16
    struct = jax.ShapeDtypeStruct
    vm, dma = pltpu.VMEM, pltpu.SemaphoreType.DMA
    meta = jnp.stack([lax.axis_index("elem"), lax.axis_index("mode")]).astype(jnp.int32)
    to_right = [(i, i + 1) for i in range(groups - 1)]
    to_left = [(i + 1, i) for i in range(groups - 1)]

    side = struct((own_rows, rim, nodes), f32)
    tail, head = call(
        pack_kernel, "pack", (side, side), (vmem, vmem), [hbm], [dma((2,))], (previous,), 60, 1
    )
    prev_left = lax.ppermute(tail, "elem", to_right)
    prev_right = lax.ppermute(head, "elem", to_left)

    odd_table, even_table = dft_tables(planes)
    half, tile = planes // 2, 64
    spectrum = call(
        functools.partial(spectrum_kernel, tile),
        "spectrum",
        (struct((devices, local, rows, nodes), f32),) * chunks,
        (hbm,) * chunks,
        [anywhere, anywhere, hbm, vmem, hbm, hbm],
        [
            vm((planes * local, nodes), f32),
            vm(odd_table.shape, bf16),
            vm(even_table.shape, bf16),
            *([vm((half, local * nodes), bf16)] * 4),
            vm((chunks, devices, local, rows, nodes), f32),
            dma((planes // 4 // tile, 4)),
            dma((2,)),
            dma((chunks, local // 2)),
        ],
        (
            tail, head, velocity.reshape(planes * local, nodes), derivative,
            jnp.asarray(odd_table), jnp.asarray(even_table),
        ),
        60,
        40,
    )
    sent = [lax.all_to_all(s, "mode", split_axis=0, concat_axis=0, tiled=True) for s in spectrum]
    rhs = [s.reshape(elems, rows, nodes) for s in sent]

    field = struct((elems, rows, nodes), f32)
    scalars = (meta, neighbours, reaction, axial_weight)
    base = []
    for c in range(chunks):
        cut = slice(c * rows, (c + 1) * rows)
        base.append(
            call(
                functools.partial(start_kernel, planes, c),
                "start",
                field,
                vmem,
                [smem] * 4 + [vmem] * 5,
                [
                    vm((elems + 2 * rim, rows, 2 * nodes), bf16),
                    vm((3, elems + 1, rows, nodes), f32),
                    vm((elems + rim + 1, rows, nodes), f32),
                    vm((elems + rim + 1, rows, nodes), f32),
                ],
                (*scalars, previous[cut], prev_left[cut], prev_right[cut], stiffness, coupling),
                24,
                80,
            )
        )
    out = None
    tails = []
    for c in range(chunks):
        edge = struct((rim, rows, nodes), f32)
        first, head, tail = call(
            functools.partial(first_kernel, planes, c),
            "first",
            (field, edge, edge),
            (vmem,) * 3,
            [smem] * 3 + [vmem] * 3,
            [],
            (meta, reaction, axial_weight, base[c], rhs[c], stiffness),
            4,
            1,
        )
        left = lax.ppermute(tail, "elem", to_right)
        right = lax.ppermute(head, "elem", to_left)
        args = (*scalars, first, rhs[c], stiffness, coupling)
        whole = struct((own_rows, elems, nodes), f32)
        out, rest = call(
            functools.partial(second_kernel, planes, c),
            "second",
            (whole, struct((2 * rim, rows, nodes), f32)),
            (hbm, vmem),
            [smem] * 4 + [vmem] * 4 + [hbm] * (out is not None),
            [
                vm((elems, rows, 2 * nodes), bf16),
                vm((5, elems + 1, rows, nodes), f32),
                vm((rows, elems - 2 * rim, nodes), f32),
                dma,
            ],
            args if out is None else (*args, out),
            24,
            20,
            None if out is None else {len(args): 0},
        )
        tails.append((rest, left, right))
    for c, (rest, left, right) in enumerate(tails):
        args = (*scalars, rest, left, right, stiffness, coupling, out)
        out = call(
            functools.partial(finish_kernel, planes, c),
            "finish",
            whole,
            hbm,
            [smem] * 4 + [vmem] * 5 + [hbm],
            [
                vm((2 * rim, rows, 2 * nodes), bf16),
                vm((2, rim + 1, rows, nodes), f32),
                vm((2, rows, rim, nodes), f32),
                dma((2,)),
            ],
            args,
            8,
            1,
            {len(args) - 1: 0},
        )
    return out


def solution(mesh):
    return jax.shard_map(
        body,
        mesh=mesh,
        in_specs=(
            P(None, ("elem", "mode"), None),
            P("mode", "elem", None),
            P(),
            P(),
            P(),
            P("elem"),
            P("elem"),
            P("elem", None),
        ),
        out_specs=P("mode", "elem", None),
        check_vma=False,
    )
```

```python
import functools
import math

import jax
import jax.numpy as jnp
import numpy as np
from jax import lax
from jax.experimental import pallas as pl
from jax.experimental.pallas import tpu as pltpu
from jax.sharding import PartitionSpec as P

dt_step = 0.5
first_weight = 0.7
second_weight = 1.1

plan = (("all", 128),)


def row_starts():
    at, starts = 0, []
    for _, rows in plan:
        starts.append(at)
        at += rows
    return starts


def split(x):
    high = x.astype(jnp.bfloat16)
    low = (x - high.astype(jnp.float32)).astype(jnp.bfloat16)
    return high, low


def pair(x):
    return jnp.concatenate(split(x), axis=1)


def pair_weight(w):
    high, low = split(w)
    return jnp.concatenate(
        [jnp.concatenate([high, high], axis=1), jnp.concatenate([low, low], axis=1)], axis=0
    )


def dot_nt(x, w):
    return lax.dot_general(x, w, (((1,), (1,)), ((), ())), preferred_element_type=jnp.float32)


def times(x, w):
    y = dot_nt(x, w)
    n = y.shape[1] // 2
    return y[:, :n] + y[:, n:]


@functools.cache
def dft_tables(planes):
    half, quarter = planes // 2, planes // 4
    rows = np.arange(planes)
    waves = np.where(rows <= half, rows, rows - half)

    def table(picked, count):
        z = np.arange(count)
        phase = (waves[picked][:, None] * z[None, :]) % planes
        angle = 2.0 * np.pi / planes * phase
        t = np.where((picked <= half)[:, None], np.cos(angle), -np.sin(angle)) * planes**-0.5
        high = t.astype(np.float32).astype(jnp.bfloat16)
        low = (t - high.astype(np.float64)).astype(np.float32).astype(jnp.bfloat16)
        return np.concatenate([high, low], axis=1)

    odd = table(rows[1::2], half)
    even = np.concatenate([table(rows[2::4], quarter), table(rows[0::4], quarter)], axis=0)
    return np.concatenate([odd, even], axis=1)


def dft3(t, h, l):
    k = t.shape[1] // 2
    dot = functools.partial(jnp.dot, preferred_element_type=jnp.float32)
    return dot(t[:, :k], h) + dot(t[:, :k], l) + dot(t[:, k:], h)


def sides(meta, elems):
    rim = elems // 4
    odd = lax.rem(meta[0], 2)
    return pl.multiple_of((1 - odd) * (elems - rim), rim), pl.multiple_of(odd * (elems - rim), rim)


def by_side(meta, make):
    odd = lax.rem(meta[0], 2)

    def each(step):
        for value in range(2):

            @pl.when(odd == value)
            def _():
                for c in make(value):
                    step(c)

    return lambda: each(lambda c: c.start()), lambda: each(lambda c: c.wait())


def side_read(meta, prev, to, sems, near):
    elems = prev.shape[1]
    rows, rim, _ = to.shape
    parts = sems.shape[0]
    n = rows // parts

    def make(odd):
        at = (odd ^ near) * (elems - rim)
        return [
            pltpu.make_async_copy(
                prev.at[i * n : (i + 1) * n, at : at + rim, :], to.at[i * n : (i + 1) * n], sems.at[i]
            )
            for i in range(parts)
        ]

    return by_side(meta, make)


def pack_kernel(meta, prev, far_out, sems):
    start, wait = side_read(meta, prev, far_out, sems, 0)
    start()
    wait()


def spectrum_kernel(tile, devices, meta, far_in, prev, vel, der, table_hbm, near_out, *refs):
    outs, (table, dh, dl, eh, el, stage, sems, table_sem, near_sems) = refs[:-9], refs[-9:]
    start_near, wait_near = side_read(meta, prev, near_out, near_sems, 1)
    table_read = pltpu.make_async_copy(table_hbm, table, table_sem)
    table_read.start()
    nodes = der.shape[0]
    local = dh.shape[1] // nodes
    planes = vel.shape[0] // local
    quarter = planes // 4
    weight = pair_weight(der[...])

    for t in range(quarter // tile):
        for e in range(local):
            cols = slice(e * nodes, (e + 1) * nodes)
            v = jnp.concatenate(
                [
                    vel[pl.ds((j * quarter + t * tile) * local + e, tile, stride=local), :]
                    for j in range(4)
                ],
                axis=0,
            )
            p = v - dt_step * v * times(pair(v), weight)
            p0, p1, p2, p3 = (p[j * tile : (j + 1) * tile] for j in range(4))
            s0, s1 = p0 + p2, p1 + p3
            here, there = slice(t * tile, (t + 1) * tile), slice(quarter + t * tile, quarter + (t + 1) * tile)
            dh[here, cols], dl[here, cols] = split(p0 - p2)
            dh[there, cols], dl[there, cols] = split(p1 - p3)
            eh[here, cols], el[here, cols] = split(s0 - s1)
            eh[there, cols], el[there, cols] = split(s0 + s1)

    table_read.wait()
    start_near()
    rows = stage.shape[2]
    group, halves = 2, 2
    writes = []
    some_devices = devices // halves
    for g in range(0, local, group):
        cols = slice(g * nodes, (g + group) * nodes)
        for half in range(halves):
            m0 = half * some_devices
            for top, ph, pl_, width, offset, stride in (
                (0, dh[:, cols], dl[:, cols], slice(0, planes), 1, 2),
                (0, eh[:quarter, cols], el[:quarter, cols], slice(planes, None), 2, 4),
                (quarter, eh[quarter:, cols], el[quarter:, cols], slice(planes, None), 0, 4),
            ):
                n = rows // stride
                values = dft3(table[top + m0 * n : top + (m0 + some_devices) * n, width], ph, pl_)
                for m in range(some_devices):
                    for e in range(group):
                        stage[m0 + m, g + e, pl.ds(offset, n, stride=stride), :] = values[
                            m * n : (m + 1) * n, e * nodes : (e + 1) * nodes
                        ]
            where = (pl.ds(m0, some_devices), pl.ds(g, group))
            writes.append(
                pltpu.make_async_copy(stage.at[where], outs[0].at[where], sems.at[half, g // group])
            )
            writes[-1].start()
    wait_near()
    for c in writes:
        c.wait()


def row_shift(first_row, count, planes, lanes):
    rows = first_row + lax.broadcasted_iota(jnp.int32, (count, lanes), 0)
    half = planes // 2
    waves = jnp.where(rows <= half, rows, rows - half).astype(jnp.float32)
    return 4.0 * (waves * (1.0 / half)) ** 2


def diagonal(stiff):
    n = stiff.shape[0]
    eye = lax.broadcasted_iota(jnp.int32, (n, n), 0) == lax.broadcasted_iota(jnp.int32, (n, n), 1)
    return jnp.sum(jnp.where(eye, stiff, 0.0), axis=0, keepdims=True)


def start_kernel(planes, row_start, meta, near, reaction, axial, prev, near_in, far_in, stiff, coupling, base, far_base, out, h, y, y0, y1, sem):
    elems, rows, nodes = base.shape
    own_rows, rim, _ = near_in.shape
    group = meta[0] * elems
    prev = prev.reshape(own_rows * elems, nodes)
    near_at, far_at = sides(meta, elems)

    for side, first in ((near_in, near_at), (far_in, far_at)):
        side = side.reshape(own_rows * rim, nodes)
        place = jnp.where(first > 0, rim + elems, 0)
        for e in range(rim):
            h[place + e] = pair(side[pl.ds(row_start * rim + e, rows, stride=rim), :])
    for e in range(elems):
        v = prev[pl.ds(row_start * elems + e, rows, stride=elems), :]
        out[e] = v
        h[rim + e] = pair(v)
    step = 8

    def fill(dst, w, a, b):
        for i in range(a, b, step):
            x = h[i : i + step].reshape(step * rows, 2 * nodes)
            dst[i - a : i - a + step] = times(x, w).reshape(step, rows, nodes)

    fill(y0, pair_weight(coupling[0]), 0, rim + elems)
    fill(y1, pair_weight(coupling[1]), rim, rim + elems + rim)
    y0[rim + elems] = jnp.zeros((rows, nodes), jnp.float32)
    y1[rim + elems] = jnp.zeros((rows, nodes), jnp.float32)
    for f in (2, 3):
        fill(y.at[f - 2], pair_weight(coupling[f]), rim, rim + elems)
        y[f - 2, elems] = jnp.zeros((rows, nodes), jnp.float32)
    fill(y.at[2], pair_weight(stiff[...]), rim, rim + elems)

    shift = row_shift(meta[1] * sum(r for _, r in plan) + row_start, rows, planes, nodes)
    diag = diagonal(stiff[...])

    def place(e, f, low, high):
        n = near[e, f]
        return jnp.where(n >= 0, jnp.clip(n - group + low, 0, high - 1), high)

    def combine(e, carry):
        v = out[e]
        scaling = reaction[e] + shift * axial[e]
        total = y[2, e] + scaling * v
        total += y0[place(e, 0, rim, rim + elems)] + y1[place(e, 1, 0, rim + elems)]
        total += y[0, place(e, 2, 0, elems)] + y[1, place(e, 3, 0, elems)]
        out[e] = v - first_weight * total / (diag + scaling)
        return carry

    lax.fori_loop(0, elems, combine, 0)
    copy = pltpu.make_async_copy(out, base, sem)
    copy.start()
    for i in range(rim):
        far_base[i] = out[far_at + i]
    copy.wait()


def edge_kernel(planes, row_start, devices, meta, reaction, axial, far_base, base_hbm, rhs, stiff, near_out, far_out, near_base, sem):
    rim, rows, nodes = far_out.shape
    local = rhs.shape[1]
    elems = local * devices
    near_at, far_at = sides(meta, elems)
    read = pltpu.make_async_copy(base_hbm.at[pl.ds(near_at, rim)], near_base, sem)
    read.start()
    shift = row_shift(meta[1] * sum(r for _, r in plan) + row_start, rows, planes, nodes)
    diag = diagonal(stiff[...])
    for base, out, at in ((far_base, far_out, far_at), (near_base, near_out, near_at)):
        source = jnp.where(at > 0, (elems - rim) // local, 0)
        if base is near_base:
            read.wait()
        for i in range(rim):
            e = at + i
            inverse = 1.0 / (diag + reaction[e] + shift * axial[e])
            out[i] = base[i] + first_weight * (rhs[source + i // local, i % local] * inverse)


def second_kernel(planes, row_start, devices, meta, near, reaction, axial, base_hbm, rhs, near_in, stiff, coupling, *refs):
    out, rest, h, y, stage, sem, first, target, base, sems = refs[-10:]
    elems, rows, nodes = first.shape
    rim = rest.shape[0]
    local = elems // devices
    done = elems - rim
    group = meta[0] * elems
    near_at, far_at = sides(meta, elems)
    reads = []
    for k in range(devices):
        part = pl.ds(k * local, local)
        reads.append(pltpu.make_async_copy(base_hbm.at[part], base.at[part], sems.at[k]))
        reads[-1].start()
    shift = row_shift(meta[1] * sum(r for _, r in plan) + row_start, rows, planes, nodes)
    diag = diagonal(stiff[...])
    for e in range(rim):
        h[elems + e] = pair(near_in[e])
    for e in range(elems):
        if e % local == 0:
            reads[e // local].wait()
        r = rhs[e // local, e % local] * (1.0 / (diag + reaction[e] + shift * axial[e]))
        v = base[e] + first_weight * r
        first[e] = v
        h[e] = pair(v)
        target[e] = v + second_weight * r
    step = 8

    def fill(f, w, to=elems):
        for i in range(0, to, step):
            y[f, i : i + step] = times(h[i : i + step].reshape(step * rows, 2 * nodes), w).reshape(step, rows, nodes)

    for f in range(4):
        fill(f, pair_weight(coupling[f]), elems + rim if f < 2 else elems)
        y[f, elems + rim] = jnp.zeros((rows, nodes), jnp.float32)
    fill(4, pair_weight(stiff[...]))
    near_first = jnp.where(near_at > 0, elems, -rim)

    def place(e, f):
        n = near[e, f]
        at = n - group
        beside = at - near_first
        is_beside = (beside >= 0) & (beside < rim)
        is_own = (at >= 0) & (at < elems)
        at = jnp.where(is_own, at, jnp.where(is_beside, elems + beside, elems + rim))
        return jnp.where(n >= 0, at, elems + rim)

    def combine(e):
        v = first[e]
        scaling = reaction[e] + shift * axial[e]
        total = y[4, e] + scaling * v
        for f in range(4):
            total += y[f, place(e, f)]
        return target[e] - second_weight * total / (diag + scaling)

    lowest = pl.multiple_of(jnp.where(far_at > 0, 0, rim), rim)
    flat = stage.reshape(rows * done, nodes)
    for i in range(done):
        flat[pl.ds(i, rows, stride=done), :] = combine(lowest + i)
    start, wait = by_side(
        meta,
        lambda odd: [
            pltpu.make_async_copy(
                stage, out.at[row_start : row_start + rows, rim * (1 - odd) : rim * (1 - odd) + done, :], sem
            )
        ],
    )
    start()
    for i in range(rim):
        rest[i] = combine(far_at + i)
    wait()


def finish_kernel(planes, row_start, meta, near, reaction, axial, rest, far_in, stiff, coupling, kept, out, h, y, stage, sems):
    elems = near.shape[0]
    rim, rows, nodes = rest.shape
    group = meta[0] * elems
    _, far_at = sides(meta, elems)
    face = jnp.where(far_at > 0, 1, 0)
    far_first = group + jnp.where(far_at > 0, elems, -rim)
    parts = h.shape[0]
    n = rows // parts
    weight = pair_weight(coupling[face])
    diag = diagonal(stiff[...])
    y[rim] = jnp.zeros((n, nodes), jnp.float32)
    copies = []
    for p in range(parts):
        for e in range(rim):
            h[p, e] = pair(far_in[e, p * n : (p + 1) * n])
        y[:rim] = times(h[p].reshape(rim * n, 2 * nodes), weight).reshape(rim, n, nodes)
        first_row = row_start + p * n
        shift = row_shift(meta[1] * sum(r for _, r in plan) + first_row, n, planes, nodes)
        flat = stage.at[p].reshape(n * rim, nodes)
        for i in range(rim):
            e = far_at + i
            number = near[e, face]
            at = number - far_first
            at = jnp.where((number >= 0) & (at >= 0) & (at < rim), at, rim)
            scaling = reaction[e] + shift * axial[e]
            flat[pl.ds(i, n, stride=rim), :] = rest[i, p * n : (p + 1) * n] - second_weight * y[at] / (diag + scaling)

        def make(odd, p=p, first_row=first_row):
            at = odd * (elems - rim)
            return [pltpu.make_async_copy(stage.at[p], out.at[first_row : first_row + n, at : at + rim, :], sems.at[p])]

        copies.append(by_side(meta, make))
        copies[-1][0]()
    for _, wait in copies:
        wait()


vmem = pl.BlockSpec(memory_space=pltpu.VMEM)
smem = pl.BlockSpec(memory_space=pltpu.SMEM)
hbm = pl.BlockSpec(memory_space=pltpu.HBM)
anywhere = pl.BlockSpec(memory_space=pl.ANY)


cost = dict(edge=(4, 1), pack=(4, 1), spectrum=(24, 40), start=(24, 60), second=(28, 15), finish=(8, 2))


def call(kernel, name, outs, out_specs, in_specs, scratch, args, mib, us, aliases=None, grid=()):
    return pl.pallas_call(
        kernel,
        out_shape=outs,
        in_specs=in_specs,
        out_specs=out_specs,
        scratch_shapes=scratch,
        compiler_params=pltpu.CompilerParams(vmem_limit_bytes=mib * 2**20),
        cost_estimate=pl.CostEstimate(flops=int(us * 1e9), bytes_accessed=int(us * 3e6), transcendentals=0),
        input_output_aliases=aliases or {},
        grid=grid,
        name=name,
    )(*args)


def body(velocity, previous, derivative, stiffness, coupling, reaction, axial_weight, neighbours):
    planes, local, nodes = velocity.shape
    own_rows, elems, _ = previous.shape
    rim = elems // 4
    devices = planes // own_rows
    groups = lax.axis_size("elem")
    f32, bf16 = jnp.float32, jnp.bfloat16
    struct = jax.ShapeDtypeStruct
    vm, dma = pltpu.VMEM, pltpu.SemaphoreType.DMA
    meta = jnp.stack([lax.axis_index("elem"), lax.axis_index("mode")]).astype(jnp.int32)
    near_pairs = [(i, i ^ 1) for i in range(groups)]
    far_pairs = [p for i in range(1, groups - 1, 2) for p in ((i, i + 1), (i + 1, i))]

    def exchange(side, pairs):
        return lax.ppermute(side, "elem", pairs)

    def fixed(x, space=pltpu.VMEM):
        return pltpu.with_memory_space_constraint(x, space)

    side = (own_rows, rim, nodes)
    far_out = call(
        pack_kernel,
        "pack",
        pltpu.VMEM(side, f32),
        vmem,
        [smem, hbm],
        [dma((4,))],
        (meta, fixed(previous, pltpu.HBM)),
        *cost["pack"],
    )
    prev_far = exchange(far_out, far_pairs)

    table = dft_tables(planes)
    half, tile = planes // 2, 64
    blocks = []
    for kind, rows in plan:
        if kind == "all":
            blocks.append(pltpu.HBM((devices, local, rows, nodes), f32))
        else:
            blocks.extend([pltpu.HBM((local, rows, nodes), f32)] * devices)
    spectrum = call(
        functools.partial(spectrum_kernel, tile, devices),
        "spectrum",
        (struct(side, f32), *blocks),
        (vmem,) + (hbm,) * len(blocks),
        [smem, vmem, hbm, vmem, vmem, hbm],
        [
            vm(table.shape, bf16),
            *([vm((half, local * nodes), bf16)] * 4),
            vm((devices, local, own_rows, nodes), f32),
            dma((2, local // 2)),
            dma,
            dma((4,)),
        ],
        (
            meta, fixed(far_out), fixed(previous, pltpu.HBM),
            velocity.reshape(planes * local, nodes), derivative,
            fixed(jnp.asarray(table), pltpu.HBM),
        ),
        *cost["spectrum"],
    )
    rhs = []
    near_out, *spectrum = spectrum
    prev_near = exchange(near_out, near_pairs)
    for kind, rows in plan:
        if kind == "all":
            rhs.append([lax.all_to_all(spectrum.pop(0), "mode", split_axis=0, concat_axis=0, tiled=True)])
        else:
            rhs.append([spectrum.pop(0)])
            for k in range(1, devices):
                rhs[-1].append(lax.ppermute(spectrum.pop(0), "mode", [(m, m ^ k) for m in range(devices)]))

    scalars = (meta, neighbours, reaction, axial_weight)
    base = []
    for (_, rows), at in zip(plan, row_starts()):
        base.append(
            call(
                functools.partial(start_kernel, planes, at),
                "start",
                (pltpu.HBM((elems, rows, nodes), f32), pltpu.VMEM((rim, rows, nodes), f32)),
                (hbm, vmem),
                [smem] * 4 + [vmem] * 5,
                [
                    vm((elems, rows, nodes), f32),
                    vm((elems + 2 * rim, rows, 2 * nodes), bf16),
                    vm((3, elems + 1, rows, nodes), f32),
                    vm((elems + rim + 1, rows, nodes), f32),
                    vm((elems + rim + 1, rows, nodes), f32),
                    dma,
                ],
                (*scalars, previous, prev_near, prev_far, stiffness, coupling),
                *cost["start"],
            )
        )
    whole = struct((own_rows, elems, nodes), f32)
    out = None
    tails = []
    for c, ((_, rows), at) in enumerate(zip(plan, row_starts())):
        field = struct((elems, rows, nodes), f32)
        edge = struct((rim, rows, nodes), f32)
        base_all, base_far = base[c]
        short = (meta, reaction, axial_weight)
        near_out, far_out = call(
            functools.partial(edge_kernel, planes, at, devices),
            "edge", (edge, edge), (vmem, vmem), [smem] * 3 + [vmem, hbm, vmem, vmem], [vm((rim, rows, nodes), f32), dma],
            (*short, fixed(base_far), fixed(base_all, pltpu.HBM), *rhs[c], stiffness),
            *cost["edge"],
        )
        near_in = exchange(near_out, near_pairs)
        far_in = exchange(far_out, far_pairs)
        args = (*scalars, fixed(base_all, pltpu.HBM), *rhs[c], near_in, stiffness, coupling)
        out, rest = call(
            functools.partial(second_kernel, planes, at, devices),
            "second",
            (whole, struct((rim, rows, nodes), f32)),
            (hbm, vmem),
            [smem] * 4 + [hbm] + [vmem] * 4 + [hbm] * (out is not None),
            [
                vm((elems + rim, rows, 2 * nodes), bf16),
                vm((5, elems + rim + 1, rows, nodes), f32),
                vm((rows, elems - rim, nodes), f32),
                dma,
                *([vm((elems, rows, nodes), f32)] * 3),
                dma((devices,)),
            ],
            args if out is None else (*args, out),
            *cost["second"],
            aliases=None if out is None else {len(args): 0},
        )
        tails.append((rows, at, rest, far_in))
    for rows, at, rest, far_in in tails:
        args = (*scalars, rest, far_in, stiffness, coupling, out)
        out = call(
            functools.partial(finish_kernel, planes, at),
            "finish",
            whole,
            hbm,
            [smem] * 4 + [vmem] * 4 + [hbm],
            [
                vm((4, rim, rows // 4, 2 * nodes), bf16),
                vm((rim + 1, rows // 4, nodes), f32),
                vm((4, rows // 4, rim, nodes), f32),
                dma((4,)),
            ],
            args,
            *cost["finish"],
            aliases={len(args) - 1: 0},
        )
    return out


def solution(mesh):
    return jax.shard_map(
        body,
        mesh=mesh,
        in_specs=(
            P(None, ("elem", "mode"), None),
            P("mode", "elem", None),
            P(),
            P(),
            P(),
            P("elem"),
            P("elem"),
            P("elem", None),
        ),
        out_specs=P("mode", "elem", None),
        check_vma=False,
    )
```

```python
import functools
import math

import jax
import jax.numpy as jnp
import numpy as np
from jax import lax
from jax.experimental import pallas as pl
from jax.experimental.pallas import tpu as pltpu
from jax.sharding import PartitionSpec as P

dt_step = 0.5
first_weight = 0.7
second_weight = 1.1

plan = (("all", 128),)


def row_starts():
    at, starts = 0, []
    for _, rows in plan:
        starts.append(at)
        at += rows
    return starts


def split(x):
    high = x.astype(jnp.bfloat16)
    low = (x - high.astype(jnp.float32)).astype(jnp.bfloat16)
    return high, low


def pair(x):
    return jnp.concatenate(split(x), axis=1)


def pair_weight(w):
    high, low = split(w)
    return jnp.concatenate(
        [jnp.concatenate([high, high], axis=1), jnp.concatenate([low, low], axis=1)], axis=0
    )


def dot_nt(x, w):
    return lax.dot_general(x, w, (((1,), (1,)), ((), ())), preferred_element_type=jnp.float32)


def times(x, w):
    y = dot_nt(x, w)
    n = y.shape[1] // 2
    return y[:, :n] + y[:, n:]


@functools.cache
def dft_tables(planes):
    half, quarter = planes // 2, planes // 4
    rows = np.arange(planes)
    waves = np.where(rows <= half, rows, rows - half)

    def table(picked, count):
        z = np.arange(count)
        phase = (waves[picked][:, None] * z[None, :]) % planes
        angle = 2.0 * np.pi / planes * phase
        t = np.where((picked <= half)[:, None], np.cos(angle), -np.sin(angle)) * planes**-0.5
        high = t.astype(np.float32).astype(jnp.bfloat16)
        low = (t - high.astype(np.float64)).astype(np.float32).astype(jnp.bfloat16)
        return np.concatenate([high, low], axis=1)

    odd = table(rows[1::2], half)
    even = np.concatenate([table(rows[2::4], quarter), table(rows[0::4], quarter)], axis=0)
    return odd, even


def dft3(t, h, l):
    k = t.shape[1] // 2
    dot = functools.partial(jnp.dot, preferred_element_type=jnp.float32)
    return dot(t[:, :k], h) + dot(t[:, :k], l) + dot(t[:, k:], h)


def sides(meta, elems):
    rim = elems // 4
    odd = lax.rem(meta[0], 2)
    return pl.multiple_of((1 - odd) * (elems - rim), rim), pl.multiple_of(odd * (elems - rim), rim)


def by_side(meta, make):
    odd = lax.rem(meta[0], 2)

    def each(step):
        for value in range(2):

            @pl.when(odd == value)
            def _():
                for c in make(value):
                    step(c)

    return lambda: each(lambda c: c.start()), lambda: each(lambda c: c.wait())


def side_read(meta, prev, to, sems, near):
    elems = prev.shape[1]
    rows, rim, _ = to.shape
    parts = sems.shape[0]
    n = rows // parts

    def make(odd):
        at = (odd ^ near) * (elems - rim)
        return [
            pltpu.make_async_copy(
                prev.at[i * n : (i + 1) * n, at : at + rim, :], to.at[i * n : (i + 1) * n], sems.at[i]
            )
            for i in range(parts)
        ]

    return by_side(meta, make)


def pack_kernel(meta, prev, far_out, sems):
    start, wait = side_read(meta, prev, far_out, sems, 0)
    start()
    wait()


def spectrum_kernel(tile, devices, meta, far_in, prev, vel, der, odd_table, even_hbm, near_out, *refs):
    outs, (even_table, dh, dl, eh, el, stage, sems, table_sem, near_sems) = refs[:-9], refs[-9:]
    start_near, wait_near = side_read(meta, prev, near_out, near_sems, 1)
    table_read = pltpu.make_async_copy(even_hbm, even_table, table_sem)
    table_read.start()
    start_near()
    nodes = der.shape[0]
    local = dh.shape[1] // nodes
    planes = vel.shape[0] // local
    quarter = planes // 4
    weight = pair_weight(der[...])

    for t in range(quarter // tile):
        for e in range(local):
            cols = slice(e * nodes, (e + 1) * nodes)
            v = jnp.concatenate(
                [
                    vel[pl.ds((j * quarter + t * tile) * local + e, tile, stride=local), :]
                    for j in range(4)
                ],
                axis=0,
            )
            p = v - dt_step * v * times(pair(v), weight)
            p0, p1, p2, p3 = (p[j * tile : (j + 1) * tile] for j in range(4))
            s0, s1 = p0 + p2, p1 + p3
            here, there = slice(t * tile, (t + 1) * tile), slice(quarter + t * tile, quarter + (t + 1) * tile)
            dh[here, cols], dl[here, cols] = split(p0 - p2)
            dh[there, cols], dl[there, cols] = split(p1 - p3)
            eh[here, cols], el[here, cols] = split(s0 - s1)
            eh[there, cols], el[there, cols] = split(s0 + s1)

    table_read.wait()
    rows = stage.shape[2]
    group, halves = 2, 2
    writes = []
    some_devices = devices // halves
    for g in range(0, local, group):
        cols = slice(g * nodes, (g + group) * nodes)
        for half in range(halves):
            m0 = half * some_devices
            for table, top, high, low, offset, stride in (
                (odd_table, 0, dh[:, cols], dl[:, cols], 1, 2),
                (even_table, 0, eh[:quarter, cols], el[:quarter, cols], 2, 4),
                (even_table, quarter, eh[quarter:, cols], el[quarter:, cols], 0, 4),
            ):
                n = rows // stride
                values = dft3(table[top + m0 * n : top + (m0 + some_devices) * n], high, low)
                for m in range(some_devices):
                    for e in range(group):
                        stage[m0 + m, g + e, pl.ds(offset, n, stride=stride), :] = values[
                            m * n : (m + 1) * n, e * nodes : (e + 1) * nodes
                        ]
            where = (pl.ds(m0, some_devices), pl.ds(g, group))
            writes.append(
                pltpu.make_async_copy(stage.at[where], outs[0].at[where], sems.at[half, g // group])
            )
            writes[-1].start()
    wait_near()
    for c in writes:
        c.wait()


def row_shift(first_row, count, planes, lanes):
    rows = first_row + lax.broadcasted_iota(jnp.int32, (count, lanes), 0)
    half = planes // 2
    waves = jnp.where(rows <= half, rows, rows - half).astype(jnp.float32)
    return 4.0 * (waves * (1.0 / half)) ** 2


def diagonal(stiff):
    n = stiff.shape[0]
    eye = lax.broadcasted_iota(jnp.int32, (n, n), 0) == lax.broadcasted_iota(jnp.int32, (n, n), 1)
    return jnp.sum(jnp.where(eye, stiff, 0.0), axis=0, keepdims=True)


def start_kernel(planes, row_start, meta, near, reaction, axial, prev, near_in, far_in, stiff, coupling, base, far_base, out, h, y, y0, y1, sem):
    elems, rows, nodes = base.shape
    own_rows, rim, _ = near_in.shape
    group = meta[0] * elems
    prev = prev.reshape(own_rows * elems, nodes)
    near_at, far_at = sides(meta, elems)

    for side, first in ((near_in, near_at), (far_in, far_at)):
        side = side.reshape(own_rows * rim, nodes)
        place = jnp.where(first > 0, rim + elems, 0)
        for e in range(rim):
            h[place + e] = pair(side[pl.ds(row_start * rim + e, rows, stride=rim), :])
    for e in range(elems):
        v = prev[pl.ds(row_start * elems + e, rows, stride=elems), :]
        out[e] = v
        h[rim + e] = pair(v)
    step = 8

    def fill(dst, w, a, b):
        for i in range(a, b, step):
            x = h[i : i + step].reshape(step * rows, 2 * nodes)
            dst[i - a : i - a + step] = times(x, w).reshape(step, rows, nodes)

    fill(y0, pair_weight(coupling[0]), 0, rim + elems)
    fill(y1, pair_weight(coupling[1]), rim, rim + elems + rim)
    y0[rim + elems] = jnp.zeros((rows, nodes), jnp.float32)
    y1[rim + elems] = jnp.zeros((rows, nodes), jnp.float32)
    for f in (2, 3):
        fill(y.at[f - 2], pair_weight(coupling[f]), rim, rim + elems)
        y[f - 2, elems] = jnp.zeros((rows, nodes), jnp.float32)
    fill(y.at[2], pair_weight(stiff[...]), rim, rim + elems)

    shift = row_shift(meta[1] * sum(r for _, r in plan) + row_start, rows, planes, nodes)
    diag = diagonal(stiff[...])

    def place(e, f, low, high):
        n = near[e, f]
        return jnp.where(n >= 0, jnp.clip(n - group + low, 0, high - 1), high)

    def combine(e, carry):
        v = out[e]
        scaling = reaction[e] + shift * axial[e]
        total = y[2, e] + scaling * v
        total += y0[place(e, 0, rim, rim + elems)] + y1[place(e, 1, 0, rim + elems)]
        total += y[0, place(e, 2, 0, elems)] + y[1, place(e, 3, 0, elems)]
        out[e] = v - first_weight * total / (diag + scaling)
        return carry

    lax.fori_loop(0, elems, combine, 0)
    copy = pltpu.make_async_copy(out, base, sem)
    copy.start()
    for i in range(rim):
        far_base[i] = out[far_at + i]
    copy.wait()


def edge_kernel(planes, row_start, devices, near, meta, reaction, axial, base_in, rhs, stiff, *refs):
    out, *refs = refs[1:] if near else refs
    rim, rows, nodes = out.shape
    local = rhs.shape[1]
    elems = local * devices
    at = sides(meta, elems)[0 if near else 1]
    base, reads = base_in, []
    if near:
        base, sems = refs
        parts = sems.shape[0]
        n = rim // parts
        for p in range(parts):
            reads.append(
                pltpu.make_async_copy(base_in.at[pl.ds(at + p * n, n)], base.at[pl.ds(p * n, n)], sems.at[p])
            )
            reads[-1].start()
    shift = row_shift(meta[1] * sum(r for _, r in plan) + row_start, rows, planes, nodes)
    diag = diagonal(stiff[...])
    source = jnp.where(at > 0, (elems - rim) // local, 0)
    for i in range(rim):
        if near and i % n == 0:
            reads[i // n].wait()
        e = at + i
        inverse = 1.0 / (diag + reaction[e] + shift * axial[e])
        out[i] = base[i] + first_weight * (rhs[source + i // local, i % local] * inverse)


def second_kernel(planes, row_start, devices, meta, near, reaction, axial, base_hbm, rhs, stiff, coupling, *refs):
    out, near_rest, far_rest, h, y, stage, sem, first, target, base, sems = refs[-11:]
    elems, rows, nodes = first.shape
    rim = far_rest.shape[0]
    local = elems // devices
    done = elems - 2 * rim
    group = meta[0] * elems
    near_at, far_at = sides(meta, elems)
    reads = []
    for k in range(devices):
        part = pl.ds(k * local, local)
        reads.append(pltpu.make_async_copy(base_hbm.at[part], base.at[part], sems.at[k]))
        reads[-1].start()
    shift = row_shift(meta[1] * sum(r for _, r in plan) + row_start, rows, planes, nodes)
    diag = diagonal(stiff[...])
    for e in range(elems):
        if e % local == 0:
            reads[e // local].wait()
        r = rhs[e // local, e % local] * (1.0 / (diag + reaction[e] + shift * axial[e]))
        v = base[e] + first_weight * r
        first[e] = v
        h[e] = pair(v)
        target[e] = v + second_weight * r
    step = 8

    def fill(f, w):
        for i in range(0, elems, step):
            y[f, i : i + step] = times(h[i : i + step].reshape(step * rows, 2 * nodes), w).reshape(step, rows, nodes)

    for f in range(4):
        fill(f, pair_weight(coupling[f]))
        y[f, elems] = jnp.zeros((rows, nodes), jnp.float32)
    fill(4, pair_weight(stiff[...]))

    def place(e, f):
        at = near[e, f] - group
        return jnp.where((at >= 0) & (at < elems), at, elems)

    def combine(e):
        v = first[e]
        scaling = reaction[e] + shift * axial[e]
        total = y[4, e] + scaling * v
        for f in range(4):
            total += y[f, place(e, f)]
        return target[e] - second_weight * total / (diag + scaling)

    flat = stage.reshape(rows * done, nodes)
    for i in range(done):
        flat[pl.ds(i, rows, stride=done), :] = combine(rim + i)
    copy = pltpu.make_async_copy(stage, out.at[row_start : row_start + rows, rim : rim + done, :], sem)
    copy.start()
    for i in range(rim):
        near_rest[i] = combine(near_at + i)
        far_rest[i] = combine(far_at + i)
    copy.wait()


def finish_kernel(planes, row_start, side, meta, near, reaction, axial, rest, beside, stiff, coupling, kept, out, h, y, stage, sems):
    elems = near.shape[0]
    rim, rows, nodes = beside.shape
    group = meta[0] * elems
    column = sides(meta, elems)[side]
    face = jnp.where(column > 0, 1, 0)
    beside_first = group + jnp.where(column > 0, elems, -rim)
    parts = h.shape[0]
    n = rows // parts
    weight = pair_weight(coupling[face])
    diag = diagonal(stiff[...])
    y[rim] = jnp.zeros((n, nodes), jnp.float32)
    copies = []
    for p in range(parts):
        for e in range(rim):
            h[p, e] = pair(beside[e, p * n : (p + 1) * n])
        y[:rim] = times(h[p].reshape(rim * n, 2 * nodes), weight).reshape(rim, n, nodes)
        first_row = row_start + p * n
        shift = row_shift(meta[1] * sum(r for _, r in plan) + first_row, n, planes, nodes)
        flat = stage.at[p].reshape(n * rim, nodes)
        for i in range(rim):
            e = column + i
            number = near[e, face]
            at = number - beside_first
            at = jnp.where((number >= 0) & (at >= 0) & (at < rim), at, rim)
            scaling = reaction[e] + shift * axial[e]
            flat[pl.ds(i, n, stride=rim), :] = rest[i, p * n : (p + 1) * n] - second_weight * y[at] / (diag + scaling)

        def make(odd, p=p, first_row=first_row):
            at = (odd ^ (1 - side)) * (elems - rim)
            return [pltpu.make_async_copy(stage.at[p], out.at[first_row : first_row + n, at : at + rim, :], sems.at[p])]

        copies.append(by_side(meta, make))
        copies[-1][0]()
    for _, wait in copies:
        wait()


vmem = pl.BlockSpec(memory_space=pltpu.VMEM)
smem = pl.BlockSpec(memory_space=pltpu.SMEM)
hbm = pl.BlockSpec(memory_space=pltpu.HBM)
anywhere = pl.BlockSpec(memory_space=pl.ANY)


cost = dict(far_edge=(4, 1), near_edge=(4, 1), pack=(4, 1), spectrum=(24, 40), start=(24, 60), second=(28, 15), finish=(8, 2))


def call(kernel, name, outs, out_specs, in_specs, scratch, args, mib, us, aliases=None, grid=()):
    return pl.pallas_call(
        kernel,
        out_shape=outs,
        in_specs=in_specs,
        out_specs=out_specs,
        scratch_shapes=scratch,
        compiler_params=pltpu.CompilerParams(vmem_limit_bytes=mib * 2**20),
        cost_estimate=pl.CostEstimate(flops=int(us * 1e9), bytes_accessed=int(us * 3e6), transcendentals=0),
        input_output_aliases=aliases or {},
        grid=grid,
        name=name,
    )(*args)


def body(velocity, previous, derivative, stiffness, coupling, reaction, axial_weight, neighbours):
    planes, local, nodes = velocity.shape
    own_rows, elems, _ = previous.shape
    rim = elems // 4
    devices = planes // own_rows
    groups = lax.axis_size("elem")
    f32, bf16 = jnp.float32, jnp.bfloat16
    struct = jax.ShapeDtypeStruct
    vm, dma = pltpu.VMEM, pltpu.SemaphoreType.DMA
    meta = jnp.stack([lax.axis_index("elem"), lax.axis_index("mode")]).astype(jnp.int32)
    near_pairs = [(i, i ^ 1) for i in range(groups)]
    far_pairs = [p for i in range(1, groups - 1, 2) for p in ((i, i + 1), (i + 1, i))]

    def exchange(side, pairs):
        return lax.ppermute(side, "elem", pairs)

    def fixed(x, space=pltpu.VMEM):
        return pltpu.with_memory_space_constraint(x, space)

    side = (own_rows, rim, nodes)
    far_out = call(
        pack_kernel,
        "pack",
        pltpu.VMEM(side, f32),
        vmem,
        [smem, hbm],
        [dma((4,))],
        (meta, fixed(previous, pltpu.HBM)),
        *cost["pack"],
    )
    prev_far = exchange(far_out, far_pairs)

    odd_table, even_table = dft_tables(planes)
    half, tile = planes // 2, 64
    blocks = []
    for kind, rows in plan:
        if kind == "all":
            blocks.append(pltpu.HBM((devices, local, rows, nodes), f32))
        else:
            blocks.extend([pltpu.HBM((local, rows, nodes), f32)] * devices)
    spectrum = call(
        functools.partial(spectrum_kernel, tile, devices),
        "spectrum",
        (struct(side, f32), *blocks),
        (vmem,) + (hbm,) * len(blocks),
        [smem, vmem, hbm, vmem, vmem, vmem, hbm],
        [
            vm(even_table.shape, bf16),
            *([vm((half, local * nodes), bf16)] * 4),
            vm((devices, local, own_rows, nodes), f32),
            dma((2, local // 2)),
            dma,
            dma((4,)),
        ],
        (
            meta, fixed(far_out), fixed(previous, pltpu.HBM),
            velocity.reshape(planes * local, nodes), derivative,
            jnp.asarray(odd_table), fixed(jnp.asarray(even_table), pltpu.HBM),
        ),
        *cost["spectrum"],
    )
    rhs = []
    near_out, *spectrum = spectrum
    prev_near = exchange(near_out, near_pairs)
    for kind, rows in plan:
        if kind == "all":
            rhs.append([lax.all_to_all(spectrum.pop(0), "mode", split_axis=0, concat_axis=0, tiled=True)])
        else:
            rhs.append([spectrum.pop(0)])
            for k in range(1, devices):
                rhs[-1].append(lax.ppermute(spectrum.pop(0), "mode", [(m, m ^ k) for m in range(devices)]))

    scalars = (meta, neighbours, reaction, axial_weight)
    base = []
    for (_, rows), at in zip(plan, row_starts()):
        base.append(
            call(
                functools.partial(start_kernel, planes, at),
                "start",
                (pltpu.HBM((elems, rows, nodes), f32), pltpu.VMEM((rim, rows, nodes), f32)),
                (hbm, vmem),
                [smem] * 4 + [vmem] * 5,
                [
                    vm((elems, rows, nodes), f32),
                    vm((elems + 2 * rim, rows, 2 * nodes), bf16),
                    vm((3, elems + 1, rows, nodes), f32),
                    vm((elems + rim + 1, rows, nodes), f32),
                    vm((elems + rim + 1, rows, nodes), f32),
                    dma,
                ],
                (*scalars, previous, prev_near, prev_far, stiffness, coupling),
                *cost["start"],
            )
        )
    whole = struct((own_rows, elems, nodes), f32)
    for c, ((_, rows), at) in enumerate(zip(plan, row_starts())):
        field = struct((elems, rows, nodes), f32)
        edge = struct((rim, rows, nodes), f32)
        base_all, base_far = base[c]
        base_all = fixed(base_all, pltpu.HBM)
        short = (meta, reaction, axial_weight)
        far_out = call(
            functools.partial(edge_kernel, planes, at, devices, False),
            "far_edge", edge, vmem, [smem] * 3 + [vmem] * 3, [], (*short, fixed(base_far), *rhs[c], stiffness),
            *cost["far_edge"],
        )
        far_in = exchange(far_out, far_pairs)
        near_out = call(
            functools.partial(edge_kernel, planes, at, devices, True),
            "near_edge", edge, vmem, [smem] * 3 + [hbm] + [vmem] * 3, [vm((rim, rows, nodes), f32), dma((4,))],
            (*short, base_all, *rhs[c], stiffness, far_out),
            *cost["near_edge"],
        )
        near_in = exchange(near_out, near_pairs)
        out, near_rest, far_rest = call(
            functools.partial(second_kernel, planes, at, devices),
            "second",
            (whole, edge, edge),
            (hbm, vmem, vmem),
            [smem] * 4 + [hbm] + [vmem] * 3,
            [
                vm((elems, rows, 2 * nodes), bf16),
                vm((5, elems + 1, rows, nodes), f32),
                vm((rows, elems - 2 * rim, nodes), f32),
                dma,
                *([vm((elems, rows, nodes), f32)] * 3),
                dma((devices,)),
            ],
            (*scalars, base_all, *rhs[c], stiffness, coupling),
            *cost["second"],
        )
        for side, (rest, beside) in enumerate(((near_rest, near_in), (far_rest, far_in))):
            args = (*scalars, rest, beside, stiffness, coupling, out)
            parts = 4
            out = call(
                functools.partial(finish_kernel, planes, at, side),
                "near_finish" if side == 0 else "far_finish",
                whole,
                hbm,
                [smem] * 4 + [vmem] * 4 + [hbm],
                [
                    vm((parts, rim, rows // parts, 2 * nodes), bf16),
                    vm((rim + 1, rows // parts, nodes), f32),
                    vm((parts, rows // parts, rim, nodes), f32),
                    dma((parts,)),
                ],
                args,
                *cost["finish"],
                aliases={len(args) - 1: 0},
            )
    return out


def solution(mesh):
    return jax.shard_map(
        body,
        mesh=mesh,
        in_specs=(
            P(None, ("elem", "mode"), None),
            P("mode", "elem", None),
            P(),
            P(),
            P(),
            P("elem"),
            P("elem"),
            P("elem", None),
        ),
        out_specs=P("mode", "elem", None),
        check_vma=False,
    )
```
